256 devices in a mesh: dom: 16 (over y, x), freq: 16 (over z, core).
Axes of the slice: x: 4, y: 4, z: 8, core: 2. Of those that a mesh axis runs over, the one named last changes fastest.
Arguments:
- voltages: float32 [512, 32768], P('freq', 'dom'), may hold values from -5 to 5
- sources: float32 [512, 32768], P('freq', 'dom'), may hold values from -20 to 20
- terminals: int32 [2, 65536], P(None, 'dom'), may hold values from 0 to 4095, as said below
- elem_current: float32 [2, 65536], P(None, 'dom'), may hold values from 0.2 to 2
- elem_charge: float32 [2, 65536], P(None, 'dom'), may hold values from 0.1 to 1
- jacobi: float32 [256, 2, 2, 32768], P('freq', None, None, 'dom'), may hold values from -1.2 to 2
Outputs:
- residual: float32 [512, 32768], P('freq', 'dom')
- newton_step: float32 [512, 32768], P('freq', 'dom')
- residual_norm: float32 [], replicated
The draws below stay inside these ranges and needn't reach their ends.
Inputs may be any that keep to these rules, and one draw needn't show every extreme that they name: `terminals`: A terminal value below 2048 is a node of the element's own partition; a value v of 2048 or more is node (v - 2048) % 128 of partition (v - 2048) // 128, one of that partition's first 128 nodes.
All inputs are finite; a program needn't handle non-finite values.
Results may differ from the reference program's by a relative error of at most 0.0003.
Values sent between devices are 32-bit elements; how exact they have to be, the bound alone decides.
No kernel may reach another device: no remote copies, remote signals or barrier semaphores. Data moves between devices by JAX's collectives and lax.ppermute only.
A program may use at most 64 MiB of HBM per device.

```python
import math
import jax
import jax.numpy as jnp
from jax import lax

S = 512
NPD = 2048
NE = 4096
NB = 128
H = 256
NODES = 32768
NBT = 2048
ELEMS = 65536
N_DOM = 16


def draw_terminals(key, part):
    first_key, other_key, remote_key, pick_key = jax.random.split(key, 4)
    first = jax.random.randint(first_key, (ELEMS,), 0, NPD)
    local_other = jax.random.randint(other_key, (ELEMS,), 0, NPD)
    remote = NPD + jax.random.randint(remote_key, (ELEMS,), 0, NBT)
    picked = jax.random.randint(pick_key, (ELEMS,), 0, 4) == 0
    second = jnp.where(picked, remote, local_other)
    first = first.at[0].set(0)
    second = second.at[0].set(NPD + NBT - 1)
    return jnp.stack([first, second]).astype(jnp.int32)


def draw_sources(key, part):
    base_key = jax.random.fold_in(key, 0)
    rows = jnp.arange(S, dtype=jnp.float32) / (S - 1)
    columns = jnp.arange(NODES, dtype=jnp.float32) / (NODES - 1)
    scale = 0.5 * (1.0 + 2.0 * rows)[:, None] * (1.0 + 2.0 * columns)[None, :]
    base = jax.random.truncated_normal(base_key, -4.0, 4.0, (S, NODES), jnp.float32)
    return (base * scale).astype(jnp.float32)


def draw_jacobi(key, part):
    keys = jax.random.split(key, 6)
    shape = (H, NODES)
    bottom = 0.5
    top = 2.0
    low_off = 0.25
    high_off = 0.6
    diag_one = jnp.exp(jax.random.uniform(keys[0], shape, jnp.float32, math.log(bottom), math.log(top)))
    diag_two = jnp.exp(jax.random.uniform(keys[1], shape, jnp.float32, math.log(bottom), math.log(top)))
    mix_one = jax.random.uniform(keys[2], shape, jnp.float32, low_off, high_off)
    mix_two = jax.random.uniform(keys[3], shape, jnp.float32, low_off, high_off)
    sign_one = jnp.where(jax.random.randint(keys[4], shape, 0, 2) == 0, -1.0, 1.0)
    sign_two = jnp.where(jax.random.randint(keys[5], shape, 0, 2) == 0, -1.0, 1.0)
    mean_diag = jnp.sqrt(diag_one * diag_two)
    off_one = sign_one * mix_one * mean_diag
    off_two = sign_two * mix_two * mean_diag
    upper = jnp.stack([diag_one, off_one], axis=1)
    lower = jnp.stack([off_two, diag_two], axis=1)
    return jnp.stack([upper, lower], axis=1).astype(jnp.float32)


def levels(stream_key, dims, cuts, least, largest):
    def one(axis_at, parts):
        heights = jax.random.uniform(jax.random.fold_in(jax.random.fold_in(stream_key, 6), axis_at), (parts,), jnp.float32, least / len(cuts), largest / len(cuts))
        return jnp.repeat(jnp.exp(heights), dims[axis_at] // parts).reshape((-1,) + (1,) * (len(dims) - axis_at - 1))

    gain = one(*cuts[0])
    for cut in cuts[1:]:
        gain = gain * one(*cut)
    return gain


def noise(key, extent, deviation, bound, cuts=(), held_as=jnp.bfloat16):
    level = levels(key, extent, cuts, -0.22, 0.18) if cuts else 1.0
    drawn = jax.random.normal(key, extent, jnp.float32) * deviation * level
    return jnp.minimum(jnp.maximum(drawn, -bound), bound).astype(held_as)


def setup_inputs(seed: int = 0) -> dict:
    splits = jax.random.split(jax.random.key(seed), 7)
    return {
        "voltages": noise(splits[0], (S, NODES), 1.0, 5.0, ((0, 16), (1, 16)), jnp.float32),
        "sources": draw_sources(jax.random.fold_in(splits[6], 71), 0),
        "terminals": draw_terminals(jax.random.fold_in(splits[6], 71), 0),
        "elem_current": jnp.clip(jnp.exp(math.log(2.0) - 2.3025851 * jax.random.uniform(splits[3], (2, ELEMS), jnp.float32) ** levels(splits[3], (2, ELEMS), ((1, 16),), -0.2, 0.2)), 0.2, 2.0),
        "elem_charge": jnp.clip(jnp.exp(math.log(1.0) - 2.3025851 * jax.random.uniform(splits[4], (2, ELEMS), jnp.float32) ** levels(splits[4], (2, ELEMS), ((1, 16),), -0.2, 0.2)), 0.1, 1.0),
        "jacobi": draw_jacobi(jax.random.fold_in(splits[6], 71), 0),
    }


trust_radius = 2.0

def transform_table(samples):
    row_index = jnp.arange(samples, dtype=jnp.int32)
    harmonic = row_index // 2
    is_sine = row_index % 2 == 1
    column = jnp.arange(samples, dtype=jnp.int32)
    order = jnp.where(harmonic == 0, jnp.where(is_sine, samples // 2, 0), harmonic)
    phase = (order[:, None] * column[None, :] % samples).astype(jnp.float32) * (2.0 * math.pi / samples)
    use_sine = is_sine & (harmonic > 0)
    values = jnp.where(use_sine[:, None], jnp.sin(phase), jnp.cos(phase))
    weight = jnp.where(harmonic == 0, math.sqrt(1.0 / samples), math.sqrt(2.0 / samples)).astype(jnp.float32)
    forward = values * weight[:, None]
    pairs = forward.reshape(samples // 2, 2, samples)
    rate = 2.0 / samples * jnp.arange(samples // 2, dtype=jnp.float32)
    derived = jnp.stack([pairs[:, 1], -pairs[:, 0]], axis=1) * rate[:, None, None]
    return jnp.concatenate([forward, derived.reshape(samples, samples)], axis=1)

def reference(voltages, sources, terminals, elem_current, elem_charge, jacobi):
    node_total = voltages.shape[1]

    def partition(totals, index):
        local_terms = lax.dynamic_slice_in_dim(terminals, index * NE, NE, 1)
        cur_params = lax.dynamic_slice_in_dim(elem_current, index * NE, NE, 1)
        chg_params = lax.dynamic_slice_in_dim(elem_charge, index * NE, NE, 1)
        border_id = local_terms - NPD
        remote = border_id // NB * NPD + border_id % NB
        global_terms = jnp.where(local_terms < NPD, index * NPD + local_terms, remote).astype(jnp.int32)
        across = voltages[:, global_terms[0]] - voltages[:, global_terms[1]]
        current = cur_params[0][None, :] * across + cur_params[1][None, :] * jnp.tanh(2.0 * across)
        charge = chg_params[0][None, :] * across + chg_params[1][None, :] * jnp.tanh(across)
        flows = jnp.stack([current, charge])
        totals = totals.at[:, :, global_terms[0]].add(flows)
        totals = totals.at[:, :, global_terms[1]].add(-flows)
        return (totals, None)
    start = jnp.zeros((2, S, node_total), jnp.float32)
    totals, unused = lax.scan(partition, start, jnp.arange(N_DOM, dtype=jnp.int32))
    table = transform_table(S)
    stacked = totals.reshape(2 * S, node_total)
    residual = jnp.dot(table, stacked, precision=lax.Precision.HIGHEST, preferred_element_type=jnp.float32) - sources
    pairs = residual.reshape(S // 2, 2, node_total)
    raw = -(jacobi[:, :, 0, :] * pairs[:, 0:1, :] + jacobi[:, :, 1, :] * pairs[:, 1:2, :])
    raw = raw.reshape(S, node_total)
    squares = jnp.sum(raw * raw)
    spread = jnp.sqrt(squares / (S * node_total) + 1e-06)
    newton_step = raw * jnp.minimum(1.0, trust_radius / spread)
    residual_norm = jnp.sqrt(jnp.sum(residual * residual))
    return (residual, newton_step, residual_norm)
```

```python
import functools
import math

import jax
import jax.numpy as jnp
import ml_dtypes
import numpy as np
from jax import lax
from jax.experimental import pallas as pl
from jax.experimental.pallas import tpu as pltpu
from jax.sharding import PartitionSpec as P

S = 512
ROWS = 32
NPD = 2048
NE = 4096
NB = 128
PARTS = 16
LANES = 128
LOW = 512
HIGHS = 8
TILE = 512

trust_radius = 2.0
BF = jnp.bfloat16
F32 = jnp.float32


def transform_table():
    row = np.arange(S)
    harmonic = row // 2
    sine = (row % 2 == 1) & (harmonic > 0)
    order = np.where(harmonic == 0, np.where(row % 2 == 1, S // 2, 0), harmonic)
    phase = (order[:, None] * np.arange(S)[None, :] % S) * (2.0 * math.pi / S)
    values = np.where(sine[:, None], np.sin(phase), np.cos(phase))
    weight = np.where(harmonic == 0, math.sqrt(1.0 / S), math.sqrt(2.0 / S))
    forward = values * weight[:, None]
    pairs = forward.reshape(S // 2, 2, S)
    rate = 2.0 / S * np.arange(S // 2)
    derived = (np.stack([pairs[:, 1], -pairs[:, 0]], axis=1) * rate[:, None, None]).reshape(S, S)
    both = np.stack([forward.reshape(S, PARTS, ROWS), derived.reshape(S, PARTS, ROWS)], axis=2)
    return both.reshape(S, 2 * S)


def split(x):
    hi = x.astype(BF)
    return hi, (x - hi.astype(F32)).astype(BF)


def element_kernel(volt_ref, border_ref, term_ref, cur_ref, chg_ref, own_ref, out_ref, table_ref, acc_ref):
    per = LOW // LANES
    for a in range(HIGHS):
        if a * LOW < NPD:
            block = volt_ref[:, a * LOW : (a + 1) * LOW]
        else:
            first = a * per - NPD // LANES
            block = jnp.concatenate([border_ref[first + k] for k in range(per)], axis=1)
        hi, lo = split(block)
        table_ref[a * ROWS : (a + 1) * ROWS, :] = hi
        table_ref[(HIGHS + a) * ROWS : (HIGHS + a + 1) * ROWS, :] = lo
    acc_ref[...] = jnp.zeros_like(acc_ref)
    low_iota = lax.broadcasted_iota(jnp.int32, (LOW, TILE), 0)
    table = table_ref[...]

    def step(i, carry):
        cols = pl.ds(pl.multiple_of(i * TILE, TILE), TILE)
        highs, hots, ends = [], [], []
        for t in range(2):
            node = term_ref[t : t + 1, cols]
            high, low = node >> 9, node & (LOW - 1)
            hot = jnp.where(low_iota == low, 1.0, 0.0).astype(BF)
            found = jnp.dot(table, hot, preferred_element_type=F32)
            value = jnp.zeros((ROWS, TILE), F32)
            for a in range(HIGHS):
                part = found[a * ROWS : (a + 1) * ROWS] + found[(HIGHS + a) * ROWS : (HIGHS + a + 1) * ROWS]
                value = jnp.where(high == a, part, value)
            highs.append(high)
            hots.append(hot)
            ends.append(value)
        across = ends[0] - ends[1]
        current = cur_ref[0:1, cols] * across + cur_ref[1:2, cols] * jnp.tanh(2.0 * across)
        charge = chg_ref[0:1, cols] * across + chg_ref[1:2, cols] * jnp.tanh(across)
        hi, lo = split(jnp.concatenate([current, charge], axis=0))
        flows = jnp.concatenate([hi, lo], axis=0)
        sides = []
        for t in range(2):
            signed = flows if t == 0 else -flows
            sides.append(
                jnp.concatenate(
                    [signed * jnp.where(highs[t] == a, 1.0, 0.0).astype(BF) for a in range(HIGHS)],
                    axis=0,
                )
            )
        acc_ref[...] += lax.dot_general(
            jnp.concatenate(sides, axis=1),
            jnp.concatenate(hots, axis=1),
            (((1,), (1,)), ((), ())),
            preferred_element_type=F32,
        )
        return carry

    lax.fori_loop(0, NE // TILE, step, 0)
    for a in range(HIGHS):
        base = a * 4 * ROWS
        total = acc_ref[base : base + 2 * ROWS, :] + acc_ref[base + 2 * ROWS : base + 4 * ROWS, :]
        for k in range(per):
            block = a * per + k
            piece = total[:, k * LANES : (k + 1) * LANES]
            if block < PARTS:
                own_ref[block] = piece
            else:
                out_ref[block - PARTS] = piece


def transform_kernel(flow_ref, high_ref, low_ref, out_ref):
    hi, lo = split(flow_ref[...])
    dot = functools.partial(jnp.dot, preferred_element_type=F32)
    out_ref[...] = dot(high_ref[...], hi) + (dot(high_ref[...], lo) + dot(low_ref[...], hi))


def step_kernel(coef_ref, src_ref, jac_ref, res_ref, raw_ref, sums_ref):
    even = lax.broadcasted_iota(jnp.int32, (ROWS, LANES), 0) % 2 == 0
    raw_sum = jnp.zeros((ROWS, LANES), F32)
    res_sum = jnp.zeros((ROWS, LANES), F32)
    for k in range(NPD // LANES):
        cols = slice(k * LANES, (k + 1) * LANES)
        res = coef_ref[k] - src_ref[:, cols]
        res_ref[:, cols] = res
        first = jnp.where(even, res, pltpu.roll(res, 1, 0))
        second = jnp.where(even, pltpu.roll(res, ROWS - 1, 0), res)
        raw = -(jac_ref[:, 0, cols] * first + jac_ref[:, 1, cols] * second)
        raw_ref[:, cols] = raw
        raw_sum += raw * raw
        res_sum += res * res
    raw_row = jnp.sum(raw_sum, axis=0, keepdims=True)
    res_row = jnp.sum(res_sum, axis=0, keepdims=True)
    half = lax.broadcasted_iota(jnp.int32, (1, LANES), 1) < LANES // 2
    row = jnp.where(half, raw_row + pltpu.roll(raw_row, LANES // 2, 1), res_row + pltpu.roll(res_row, LANES // 2, 1))
    sums_ref[...] = jnp.broadcast_to(row, sums_ref.shape)


def scale_kernel(raw_ref, sums_ref, out_ref, norm_ref):
    row = jnp.sum(sums_ref[...], axis=0, keepdims=True)
    half = lax.broadcasted_iota(jnp.int32, (1, LANES), 1) < LANES // 2
    raw_sum = jnp.sum(jnp.where(half, row, 0.0), axis=1, keepdims=True)
    res_sum = jnp.sum(jnp.where(half, 0.0, row), axis=1, keepdims=True)
    spread = jnp.sqrt(raw_sum / (S * NPD * PARTS) + 1e-06)
    out_ref[...] = raw_ref[...] * jnp.minimum(1.0, trust_radius / spread)
    norm_ref[...] = jnp.sqrt(res_sum)


def call(kernel, out_shapes, scratch=(), limit=None):
    return pl.pallas_call(
        kernel,
        out_shape=[jax.ShapeDtypeStruct(s, F32) for s in out_shapes],
        scratch_shapes=list(scratch),
        compiler_params=pltpu.CompilerParams(vmem_limit_bytes=limit),
    )


def body(voltages, sources, terminals, elem_current, elem_charge, jacobi):
    sent = jnp.broadcast_to(voltages[None, :, :NB], (PARTS, ROWS, NB))
    border = lax.all_to_all(sent, "dom", 0, 0, tiled=True)
    own, outgoing = call(
        element_kernel,
        [(PARTS, 2 * ROWS, LANES), (PARTS, 2 * ROWS, LANES)],
        [pltpu.VMEM((2 * HIGHS * ROWS, LOW), BF), pltpu.VMEM((HIGHS * 4 * ROWS, LOW), F32)],
        40 * 2**20,
    )(voltages, border, terminals, elem_current, elem_charge)
    incoming = lax.all_to_all(outgoing, "dom", 0, 0, tiled=True)
    own = own.at[0].add(jnp.sum(incoming, axis=0))
    flows = lax.all_to_all(own, "freq", 0, 0, tiled=True).reshape(2 * S, LANES)
    table = transform_table()
    high = table.astype(ml_dtypes.bfloat16)
    low = (table - high.astype(np.float64)).astype(ml_dtypes.bfloat16)
    (coef,) = call(transform_kernel, [(S, LANES)], (), 24 * 2**20)(flows, jnp.asarray(high), jnp.asarray(low))
    coef = lax.all_to_all(coef.reshape(PARTS, ROWS, LANES), "freq", 0, 0, tiled=True)
    residual, raw, sums = call(step_kernel, [(ROWS, NPD), (ROWS, NPD), (256, LANES)], (), 24 * 2**20)(
        coef, sources, jacobi.reshape(ROWS, 2, NPD)
    )
    sums = lax.all_to_all(sums, ("dom", "freq"), 0, 0, tiled=True)
    newton_step, norm = call(scale_kernel, [(ROWS, NPD), (1, 1)], (), 24 * 2**20)(raw, sums)
    return residual, newton_step, norm.reshape(())


def solution(mesh):
    placed = (
        P("freq", "dom"),
        P("freq", "dom"),
        P(None, "dom"),
        P(None, "dom"),
        P(None, "dom"),
        P("freq", None, None, "dom"),
    )
    return jax.shard_map(
        body,
        mesh=mesh,
        in_specs=placed,
        out_specs=(P("freq", "dom"), P("freq", "dom"), P()),
        check_vma=False,
    )
```

```python
import functools
import math

import jax
import jax.numpy as jnp
import ml_dtypes
import numpy as np
from jax import lax
from jax.experimental import pallas as pl
from jax.experimental.pallas import tpu as pltpu
from jax.sharding import PartitionSpec as P

S = 512
ROWS = 32
NPD = 2048
NE = 4096
NB = 128
PARTS = 16
LANES = 128
LOW = 512
SHIFT = 9
HIGHS = NPD // LOW
PER = LOW // LANES
TILE = 1024

trust_radius = 2.0
BF = jnp.bfloat16
F32 = jnp.float32


def transform_table():
    row = np.arange(S)
    harmonic = row // 2
    sine = (row % 2 == 1) & (harmonic > 0)
    order = np.where(harmonic == 0, np.where(row % 2 == 1, S // 2, 0), harmonic)
    phase = (order[:, None] * np.arange(S)[None, :] % S) * (2.0 * math.pi / S)
    values = np.where(sine[:, None], np.sin(phase), np.cos(phase))
    weight = np.where(harmonic == 0, math.sqrt(1.0 / S), math.sqrt(2.0 / S))
    forward = values * weight[:, None]
    pairs = forward.reshape(S // 2, 2, S)
    rate = 2.0 / S * np.arange(S // 2)
    derived = (np.stack([pairs[:, 1], -pairs[:, 0]], axis=1) * rate[:, None, None]).reshape(S, S)
    both = np.stack([forward.reshape(S, PARTS, ROWS), derived.reshape(S, PARTS, ROWS)], axis=2)
    return both.reshape(S, 2 * S)


def split(x):
    hi = x.astype(BF)
    return hi, (x - hi.astype(F32)).astype(BF)


def one_hot(low):
    rows = lax.broadcasted_iota(jnp.int32, (256, low.shape[1]), 0).astype(F32).astype(BF)
    parts = []
    for first in range(0, LOW, 256):
        offset = jnp.broadcast_to((low - first).astype(F32).astype(BF), rows.shape)
        parts.append(jnp.where(rows == offset, jnp.ones((), BF), jnp.zeros((), BF)))
    return jnp.concatenate(parts, axis=0)


def fill_table(blocks, table_ref):
    for a, block in enumerate(blocks):
        hi, lo = split(block)
        table_ref[a * ROWS : (a + 1) * ROWS, :] = hi
        table_ref[(HIGHS + a) * ROWS : (HIGHS + a + 1) * ROWS, :] = lo


def gather(table_ref, high, hot):
    found = jnp.dot(table_ref[...], hot, preferred_element_type=F32)
    value = jnp.zeros((ROWS, hot.shape[1]), F32)
    for a in range(HIGHS):
        part = found[a * ROWS : (a + 1) * ROWS] + found[(HIGHS + a) * ROWS : (HIGHS + a + 1) * ROWS]
        value = jnp.where(high == a, part, value)
    return value


def scatter(flows, highs, hots):
    sides = []
    for t in range(2):
        signed = flows if t == 0 else -flows
        sides += [
            jnp.concatenate(
                [signed * jnp.where(highs[t] == a, 1.0, 0.0).astype(BF) for a in range(HIGHS)], axis=0
            )
        ]
    return lax.dot_general(
        jnp.concatenate(sides, axis=1),
        jnp.concatenate(hots, axis=1),
        (((1,), (1,)), ((), ())),
        preferred_element_type=F32,
    )


def put_blocks(acc_ref, out_ref):
    for a in range(HIGHS):
        base = a * 4 * ROWS
        total = acc_ref[base : base + 2 * ROWS, :] + acc_ref[base + 2 * ROWS : base + 4 * ROWS, :]
        for k in range(PER):
            out_ref[a * PER + k] = total[:, k * LANES : (k + 1) * LANES]


def tiles():
    return [slice(first, first + TILE) for first in range(0, NE, TILE)]


def own_across_kernel(volt_ref, term_ref, across_ref, table_ref):
    fill_table([volt_ref[:, a * LOW : (a + 1) * LOW] for a in range(HIGHS)], table_ref)
    for cols in tiles():
        ends = []
        for t in range(2):
            node = term_ref[t : t + 1, cols]
            ends.append(gather(table_ref, node >> SHIFT, one_hot(node & (LOW - 1))))
        across_ref[:, cols] = ends[0] - ends[1]


def flow_kernel(border_ref, across_ref, term_ref, cur_ref, chg_ref, out_ref, flows_ref, table_ref, acc_ref):
    blocks = [
        jnp.concatenate([border_ref[a * PER + k] for k in range(PER)], axis=1) for a in range(HIGHS)
    ]
    fill_table(blocks, table_ref)
    for i, cols in enumerate(tiles()):
        highs, hots, ends = [], [], []
        for t in range(2):
            node = term_ref[t : t + 1, cols]
            highs.append((node >> SHIFT) - HIGHS)
            hots.append(one_hot(node & (LOW - 1)))
            ends.append(gather(table_ref, highs[t], hots[t]))
        across = across_ref[:, cols] + (ends[0] - ends[1])
        current = cur_ref[0:1, cols] * across + cur_ref[1:2, cols] * jnp.tanh(2.0 * across)
        charge = chg_ref[0:1, cols] * across + chg_ref[1:2, cols] * jnp.tanh(across)
        flows = jnp.concatenate(split(jnp.concatenate([current, charge], axis=0)), axis=0)
        flows_ref[:, cols] = flows
        part = scatter(flows, highs, hots)
        acc_ref[...] = part if i == 0 else acc_ref[...] + part
    put_blocks(acc_ref, out_ref)


def own_flow_kernel(flows_ref, term_ref, own_ref, acc_ref):
    for i, cols in enumerate(tiles()):
        highs, hots = [], []
        for t in range(2):
            node = term_ref[t : t + 1, cols]
            highs.append(node >> SHIFT)
            hots.append(one_hot(node & (LOW - 1)))
        part = scatter(flows_ref[:, cols], highs, hots)
        acc_ref[...] = part if i == 0 else acc_ref[...] + part
    put_blocks(acc_ref, own_ref)


def transform_kernel(flow_ref, high_ref, low_ref, out_ref):
    hi, lo = split(flow_ref[...])
    dot = functools.partial(jnp.dot, preferred_element_type=F32)
    out_ref[...] = dot(high_ref[...], hi) + (dot(high_ref[...], lo) + dot(low_ref[...], hi))


def step_kernel(coef_ref, src_ref, jac_ref, res_ref, raw_ref, sums_ref):
    even = lax.broadcasted_iota(jnp.int32, (ROWS, LANES), 0) % 2 == 0
    raw_sum = jnp.zeros((ROWS, LANES), F32)
    res_sum = jnp.zeros((ROWS, LANES), F32)
    for k in range(NPD // LANES):
        cols = slice(k * LANES, (k + 1) * LANES)
        res = coef_ref[k] - src_ref[:, cols]
        res_ref[:, cols] = res
        first = jnp.where(even, res, pltpu.roll(res, 1, 0))
        second = jnp.where(even, pltpu.roll(res, ROWS - 1, 0), res)
        raw = -(jac_ref[:, 0, cols] * first + jac_ref[:, 1, cols] * second)
        raw_ref[:, cols] = raw
        raw_sum += raw * raw
        res_sum += res * res
    raw_row = jnp.sum(raw_sum, axis=0, keepdims=True)
    res_row = jnp.sum(res_sum, axis=0, keepdims=True)
    half = lax.broadcasted_iota(jnp.int32, (1, LANES), 1) < LANES // 2
    row = jnp.where(half, raw_row + pltpu.roll(raw_row, LANES // 2, 1), res_row + pltpu.roll(res_row, LANES // 2, 1))
    sums_ref[...] = jnp.broadcast_to(row, sums_ref.shape)


def scale_kernel(raw_ref, sums_ref, out_ref, norm_ref):
    row = jnp.sum(sums_ref[...], axis=0, keepdims=True)
    half = lax.broadcasted_iota(jnp.int32, (1, LANES), 1) < LANES // 2
    raw_sum = jnp.sum(jnp.where(half, row, 0.0), axis=1, keepdims=True)
    res_sum = jnp.sum(jnp.where(half, 0.0, row), axis=1, keepdims=True)
    spread = jnp.sqrt(raw_sum / (S * NPD * PARTS) + 1e-06)
    out_ref[...] = raw_ref[...] * jnp.minimum(1.0, trust_radius / spread)
    norm_ref[...] = jnp.sqrt(res_sum)


def call(kernel, out_shapes, scratch=(), limit=24, flops=0, types=None):
    types = types or [F32] * len(out_shapes)
    return pl.pallas_call(
        kernel,
        out_shape=[jax.ShapeDtypeStruct(s, t) for s, t in zip(out_shapes, types, strict=True)],
        scratch_shapes=list(scratch),
        compiler_params=pltpu.CompilerParams(vmem_limit_bytes=limit * 2**20),
        cost_estimate=pl.CostEstimate(flops=flops, bytes_accessed=2**20, transcendentals=0) if flops else None,
    )


def body(voltages, sources, terminals, elem_current, elem_charge, jacobi):
    sent = jnp.broadcast_to(voltages[None, :, :NB], (PARTS, ROWS, NB))
    border = lax.all_to_all(sent, "dom", 0, 0, tiled=True)
    table_scratch = pltpu.VMEM((2 * HIGHS * ROWS, LOW), BF)
    acc_scratch = pltpu.VMEM((HIGHS * 4 * ROWS, LOW), F32)
    (across,) = call(own_across_kernel, [(ROWS, NE)], [table_scratch], 32, 4 * 10**9)(voltages, terminals)
    outgoing, flows = call(
        flow_kernel,
        [(PARTS, 2 * ROWS, LANES), (4 * ROWS, NE)],
        [table_scratch, acc_scratch],
        40,
        8 * 10**9,
        [F32, BF],
    )(border, across, terminals, elem_current, elem_charge)
    incoming = lax.all_to_all(outgoing, "dom", 0, 0, tiled=True)
    (own,) = call(own_flow_kernel, [(PARTS, 2 * ROWS, LANES)], [acc_scratch], 32, 6 * 10**9)(flows, terminals)
    own = own.at[0].add(jnp.sum(incoming, axis=0))
    flows = lax.all_to_all(own, "freq", 0, 0, tiled=True).reshape(2 * S, LANES)
    table = transform_table()
    high = table.astype(ml_dtypes.bfloat16)
    low = (table - high.astype(np.float64)).astype(ml_dtypes.bfloat16)
    (coef,) = call(transform_kernel, [(S, LANES)], )(flows, jnp.asarray(high), jnp.asarray(low))
    coef = lax.all_to_all(coef.reshape(PARTS, ROWS, LANES), "freq", 0, 0, tiled=True)
    residual, raw, sums = call(step_kernel, [(ROWS, NPD), (ROWS, NPD), (256, LANES)], )(
        coef, sources, jacobi.reshape(ROWS, 2, NPD)
    )
    sums = lax.all_to_all(sums, ("dom", "freq"), 0, 0, tiled=True)
    newton_step, norm = call(scale_kernel, [(ROWS, NPD), (1, 1)], )(raw, sums)
    return residual, newton_step, norm.reshape(())


def solution(mesh):
    placed = (
        P("freq", "dom"),
        P("freq", "dom"),
        P(None, "dom"),
        P(None, "dom"),
        P(None, "dom"),
        P("freq", None, None, "dom"),
    )
    return jax.shard_map(
        body,
        mesh=mesh,
        in_specs=placed,
        out_specs=(P("freq", "dom"), P("freq", "dom"), P()),
        check_vma=False,
    )
```

```python
import functools
import math

import jax
import jax.numpy as jnp
import ml_dtypes
import numpy as np
from jax import lax
from jax.experimental import pallas as pl
from jax.experimental.pallas import tpu as pltpu
from jax.sharding import PartitionSpec as P

S = 512
ROWS = 32
NPD = 2048
NE = 4096
NB = 128
PARTS = 16
LANES = 128
LOW = 512
SHIFT = 9
HIGHS = NPD // LOW
PER = LOW // LANES
TILE = 1024

trust_radius = 2.0
BF = jnp.bfloat16
F32 = jnp.float32


def transform_table():
    row = np.arange(S)
    harmonic = row // 2
    sine = (row % 2 == 1) & (harmonic > 0)
    order = np.where(harmonic == 0, np.where(row % 2 == 1, S // 2, 0), harmonic)
    phase = (order[:, None] * np.arange(S)[None, :] % S) * (2.0 * math.pi / S)
    values = np.where(sine[:, None], np.sin(phase), np.cos(phase))
    weight = np.where(harmonic == 0, math.sqrt(1.0 / S), math.sqrt(2.0 / S))
    forward = values * weight[:, None]
    pairs = forward.reshape(S // 2, 2, S)
    rate = 2.0 / S * np.arange(S // 2)
    derived = (np.stack([pairs[:, 1], -pairs[:, 0]], axis=1) * rate[:, None, None]).reshape(S, S)
    both = np.stack([forward.reshape(S, PARTS, ROWS), derived.reshape(S, PARTS, ROWS)], axis=2)
    return both.reshape(S, 2 * S)


def split(x):
    hi = x.astype(BF)
    return hi, (x - hi.astype(F32)).astype(BF)


def one_hot(low):
    rows = lax.broadcasted_iota(jnp.int32, (256, low.shape[1]), 0).astype(F32).astype(BF)
    parts = []
    for first in range(0, LOW, 256):
        offset = jnp.broadcast_to((low - first).astype(F32).astype(BF), rows.shape)
        parts.append(jnp.where(rows == offset, jnp.ones((), BF), jnp.zeros((), BF)))
    return jnp.concatenate(parts, axis=0)


def fill_table(blocks, table_ref):
    for a, block in enumerate(blocks):
        hi, lo = split(block)
        table_ref[a * ROWS : (a + 1) * ROWS, :] = hi
        table_ref[(HIGHS + a) * ROWS : (HIGHS + a + 1) * ROWS, :] = lo


def gather(table_ref, high, hot):
    found = jnp.dot(table_ref[...], hot, preferred_element_type=F32)
    value = jnp.zeros((ROWS, hot.shape[1]), F32)
    for a in range(HIGHS):
        part = found[a * ROWS : (a + 1) * ROWS] + found[(HIGHS + a) * ROWS : (HIGHS + a + 1) * ROWS]
        value = jnp.where(high == a, part, value)
    return value


def lane_gather(border_ref, node):
    groups = range(0, ROWS, 8)
    columns = []
    for first in range(0, node.shape[1], LANES):
        here = jnp.broadcast_to(node[:, first : first + LANES], (8, LANES))
        block, lane = (here >> 7) - PARTS, here & (LANES - 1)
        values = [jnp.zeros((8, LANES), F32) for _ in groups]
        for p in range(PARTS):
            match = block == p
            for i, r in enumerate(groups):
                found = jnp.take_along_axis(border_ref[p, r : r + 8, :], lane, axis=1)
                values[i] = jnp.where(match, found, values[i])
        columns.append(jnp.concatenate(values, axis=0))
    return jnp.concatenate(columns, axis=1)


def scatter(flows, highs, hots):
    sides = []
    for t in range(2):
        signed = flows if t == 0 else -flows
        sides += [
            jnp.concatenate(
                [signed * jnp.where(highs[t] == a, 1.0, 0.0).astype(BF) for a in range(HIGHS)], axis=0
            )
        ]
    return lax.dot_general(
        jnp.concatenate(sides, axis=1),
        jnp.concatenate(hots, axis=1),
        (((1,), (1,)), ((), ())),
        preferred_element_type=F32,
    )


def put_blocks(acc_ref, out_ref):
    for a in range(HIGHS):
        base = a * 4 * ROWS
        total = acc_ref[base : base + 2 * ROWS, :] + acc_ref[base + 2 * ROWS : base + 4 * ROWS, :]
        for k in range(PER):
            out_ref[a * PER + k] = total[:, k * LANES : (k + 1) * LANES]


def tiles():
    return [slice(first, first + TILE) for first in range(0, NE, TILE)]


def own_across_kernel(volt_ref, term_ref, across_ref, table_ref):
    fill_table([volt_ref[:, a * LOW : (a + 1) * LOW] for a in range(HIGHS)], table_ref)
    for cols in tiles():
        ends = []
        for t in range(2):
            node = term_ref[t : t + 1, cols]
            ends.append(gather(table_ref, node >> SHIFT, one_hot(node & (LOW - 1))))
        across_ref[:, cols] = ends[0] - ends[1]


def flow_kernel(border_ref, across_ref, term_ref, cur_ref, chg_ref, out_ref, flows_ref, table_ref, acc_ref, keep_ref, sems):
    blocks = [
        jnp.concatenate([border_ref[a * PER + k] for k in range(PER)], axis=1) for a in range(HIGHS)
    ]
    fill_table(blocks, table_ref)
    copies = []

    def front(i):
        cols = tiles()[i]
        highs, hots, ends = [], [], []
        for t in range(2):
            node = term_ref[t : t + 1, cols]
            highs.append((node >> SHIFT) - HIGHS)
            hots.append(one_hot(node & (LOW - 1)))
            ends.append(lane_gather(border_ref, node) if i else gather(table_ref, highs[t], hots[t]))
        across = across_ref[:, cols] + (ends[0] - ends[1])
        current = cur_ref[0:1, cols] * across + cur_ref[1:2, cols] * jnp.tanh(2.0 * across)
        charge = chg_ref[0:1, cols] * across + chg_ref[1:2, cols] * jnp.tanh(across)
        flows = jnp.concatenate(split(jnp.concatenate([current, charge], axis=0)), axis=0)
        keep_ref[:, cols] = flows
        copies.append(pltpu.make_async_copy(keep_ref.at[:, cols], flows_ref.at[:, cols], sems.at[i]))
        copies[i].start()
        return flows, highs, hots

    count = NE // TILE
    now = front(0)
    for i in range(count):
        later = front(i + 1) if i + 1 < count else None
        part = scatter(*now)
        acc_ref[...] = part if i == 0 else acc_ref[...] + part
        now = later
    put_blocks(acc_ref, out_ref)
    for copy in copies:
        copy.wait()


def own_flow_kernel(flows_ref, term_ref, own_ref, acc_ref, keep_ref, sems):
    copies = [
        pltpu.make_async_copy(flows_ref.at[:, cols], keep_ref.at[:, cols], sems.at[i])
        for i, cols in enumerate(tiles())
    ]
    for copy in copies:
        copy.start()
    for i, cols in enumerate(tiles()):
        highs, hots = [], []
        for t in range(2):
            node = term_ref[t : t + 1, cols]
            highs.append(node >> SHIFT)
            hots.append(one_hot(node & (LOW - 1)))
        copies[i].wait()
        part = scatter(keep_ref[:, cols], highs, hots)
        acc_ref[...] = part if i == 0 else acc_ref[...] + part
    put_blocks(acc_ref, own_ref)


def transform_kernel(flow_ref, high_ref, low_ref, out_ref):
    hi, lo = split(flow_ref[...])
    dot = functools.partial(jnp.dot, preferred_element_type=F32)
    out_ref[...] = dot(high_ref[...], hi) + (dot(high_ref[...], lo) + dot(low_ref[...], hi))


def step_kernel(coef_ref, src_ref, jac_ref, res_ref, raw_ref, sums_ref):
    even = lax.broadcasted_iota(jnp.int32, (ROWS, LANES), 0) % 2 == 0
    raw_sum = jnp.zeros((ROWS, LANES), F32)
    res_sum = jnp.zeros((ROWS, LANES), F32)
    for k in range(NPD // LANES):
        cols = slice(k * LANES, (k + 1) * LANES)
        res = coef_ref[k] - src_ref[:, cols]
        res_ref[:, cols] = res
        first = jnp.where(even, res, pltpu.roll(res, 1, 0))
        second = jnp.where(even, pltpu.roll(res, ROWS - 1, 0), res)
        raw = -(jac_ref[:, 0, cols] * first + jac_ref[:, 1, cols] * second)
        raw_ref[:, cols] = raw
        raw_sum += raw * raw
        res_sum += res * res
    raw_row = jnp.sum(raw_sum, axis=0, keepdims=True)
    res_row = jnp.sum(res_sum, axis=0, keepdims=True)
    half = lax.broadcasted_iota(jnp.int32, (1, LANES), 1) < LANES // 2
    row = jnp.where(half, raw_row + pltpu.roll(raw_row, LANES // 2, 1), res_row + pltpu.roll(res_row, LANES // 2, 1))
    sums_ref[...] = jnp.broadcast_to(row, sums_ref.shape)


def scale_kernel(raw_ref, sums_ref, out_ref, norm_ref):
    row = jnp.sum(sums_ref[...], axis=0, keepdims=True)
    half = lax.broadcasted_iota(jnp.int32, (1, LANES), 1) < LANES // 2
    raw_sum = jnp.sum(jnp.where(half, row, 0.0), axis=1, keepdims=True)
    res_sum = jnp.sum(jnp.where(half, 0.0, row), axis=1, keepdims=True)
    spread = jnp.sqrt(raw_sum / (S * NPD * PARTS) + 1e-06)
    out_ref[...] = raw_ref[...] * jnp.minimum(1.0, trust_radius / spread)
    norm_ref[...] = jnp.sqrt(res_sum)


def call(kernel, out_shapes, scratch=(), limit=24, flops=0, types=None, inside=None, outside=None):
    types = types or [F32] * len(out_shapes)
    spaces = {}
    if inside:
        spaces["in_specs"] = [pl.BlockSpec(memory_space=m) for m in inside]
    if outside:
        spaces["out_specs"] = [pl.BlockSpec(memory_space=m) for m in outside]
    return pl.pallas_call(
        kernel,
        out_shape=[jax.ShapeDtypeStruct(s, t) for s, t in zip(out_shapes, types, strict=True)],
        scratch_shapes=list(scratch),
        compiler_params=pltpu.CompilerParams(vmem_limit_bytes=limit * 2**20),
        cost_estimate=pl.CostEstimate(flops=flops, bytes_accessed=2**20, transcendentals=0) if flops else None,
        **spaces,
    )


def repeat_kernel(block_ref, out_ref):
    block = block_ref[...]
    for p in range(PARTS):
        out_ref[p] = block


def body(voltages, sources, terminals, elem_current, elem_charge, jacobi):
    sent = pl.pallas_call(
        repeat_kernel,
        out_shape=jax.ShapeDtypeStruct((PARTS, ROWS, NB), F32),
        grid=(1,),
        in_specs=[pl.BlockSpec((ROWS, NB), lambda i: (0, 0))],
        out_specs=pl.BlockSpec((PARTS, ROWS, NB), lambda i: (0, 0, 0)),
    )(voltages)
    border = lax.all_to_all(sent, "dom", 0, 0, tiled=True)
    table_scratch = pltpu.VMEM((2 * HIGHS * ROWS, LOW), BF)
    acc_scratch = pltpu.VMEM((HIGHS * 4 * ROWS, LOW), F32)
    keep = [pltpu.VMEM((4 * ROWS, NE), BF), pltpu.SemaphoreType.DMA((NE // TILE,))]
    (across,) = call(own_across_kernel, [(ROWS, NE)], [table_scratch], 32, 4 * 10**9)(voltages, terminals)
    outgoing, flows = call(
        flow_kernel,
        [(PARTS, 2 * ROWS, LANES), (4 * ROWS, NE)],
        [table_scratch, acc_scratch, *keep],
        40,
        8 * 10**9,
        [F32, BF],
        None,
        [pltpu.VMEM, pltpu.HBM],
    )(border, across, terminals, elem_current, elem_charge)
    own_call = call(
        own_flow_kernel,
        [(PARTS, 2 * ROWS, LANES)],
        [acc_scratch, *keep],
        32,
        6 * 10**9,
        None,
        [pltpu.HBM, pltpu.VMEM],
    )
    (own,) = own_call(flows, terminals)
    incoming = lax.all_to_all(outgoing, "dom", 0, 0, tiled=True)
    own = own.at[0].add(jnp.sum(incoming, axis=0))
    flows = lax.all_to_all(own, "freq", 0, 0, tiled=True).reshape(2 * S, LANES)
    table = transform_table()
    high = table.astype(ml_dtypes.bfloat16)
    low = (table - high.astype(np.float64)).astype(ml_dtypes.bfloat16)
    (coef,) = call(transform_kernel, [(S, LANES)], )(flows, jnp.asarray(high), jnp.asarray(low))
    coef = lax.all_to_all(coef.reshape(PARTS, ROWS, LANES), "freq", 0, 0, tiled=True)
    residual, raw, sums = call(step_kernel, [(ROWS, NPD), (ROWS, NPD), (256, LANES)], )(
        coef, sources, jacobi.reshape(ROWS, 2, NPD)
    )
    sums = lax.all_to_all(sums, ("dom", "freq"), 0, 0, tiled=True)
    newton_step, norm = call(scale_kernel, [(ROWS, NPD), (1, 1)], )(raw, sums)
    return residual, newton_step, norm.reshape(())


def solution(mesh):
    placed = (
        P("freq", "dom"),
        P("freq", "dom"),
        P(None, "dom"),
        P(None, "dom"),
        P(None, "dom"),
        P("freq", None, None, "dom"),
    )
    return jax.shard_map(
        body,
        mesh=mesh,
        in_specs=placed,
        out_specs=(P("freq", "dom"), P("freq", "dom"), P()),
        check_vma=False,
    )
```

```python
import functools
import math

import jax
import jax.numpy as jnp
import ml_dtypes
import numpy as np
from jax import lax
from jax.experimental import pallas as pl
from jax.experimental.pallas import tpu as pltpu
from jax.sharding import PartitionSpec as P

S = 512
ROWS = 32
NPD = 2048
NE = 4096
NB = 128
PARTS = 16
LANES = 128
LOW = 512
SHIFT = 9
HIGHS = NPD // LOW
PER = LOW // LANES
TILE = 1024

trust_radius = 2.0
BF = jnp.bfloat16
F32 = jnp.float32


def transform_table():
    row = np.arange(S)
    harmonic = row // 2
    sine = (row % 2 == 1) & (harmonic > 0)
    order = np.where(harmonic == 0, np.where(row % 2 == 1, S // 2, 0), harmonic)
    phase = (order[:, None] * np.arange(S)[None, :] % S) * (2.0 * math.pi / S)
    values = np.where(sine[:, None], np.sin(phase), np.cos(phase))
    weight = np.where(harmonic == 0, math.sqrt(1.0 / S), math.sqrt(2.0 / S))
    forward = values * weight[:, None]
    pairs = forward.reshape(S // 2, 2, S)
    rate = 2.0 / S * np.arange(S // 2)
    derived = (np.stack([pairs[:, 1], -pairs[:, 0]], axis=1) * rate[:, None, None]).reshape(S, S)
    both = np.stack([forward.reshape(S, PARTS, ROWS), derived.reshape(S, PARTS, ROWS)], axis=2)
    return both.reshape(S, 2 * S)


def split(x):
    hi = x.astype(BF)
    return hi, (x - hi.astype(F32)).astype(BF)


def one_hot(low):
    rows = lax.broadcasted_iota(jnp.int32, (256, low.shape[1]), 0).astype(F32).astype(BF)
    parts = []
    for first in range(0, LOW, 256):
        offset = jnp.broadcast_to((low - first).astype(F32).astype(BF), rows.shape)
        parts.append(jnp.where(rows == offset, jnp.ones((), BF), jnp.zeros((), BF)))
    return jnp.concatenate(parts, axis=0)


def fill_table(blocks, table_ref):
    for a, block in enumerate(blocks):
        hi, lo = split(block)
        table_ref[a * ROWS : (a + 1) * ROWS, :] = hi
        table_ref[(HIGHS + a) * ROWS : (HIGHS + a + 1) * ROWS, :] = lo


def gather(table_ref, high, hot):
    found = jnp.dot(table_ref[...], hot, preferred_element_type=F32)
    value = jnp.zeros((ROWS, hot.shape[1]), F32)
    for a in range(HIGHS):
        part = found[a * ROWS : (a + 1) * ROWS] + found[(HIGHS + a) * ROWS : (HIGHS + a + 1) * ROWS]
        value = jnp.where(high == a, part, value)
    return value


def lane_gather(border_ref, node):
    groups = range(0, ROWS, 8)
    columns = []
    for first in range(0, node.shape[1], LANES):
        here = jnp.broadcast_to(node[:, first : first + LANES], (8, LANES))
        block, lane = (here >> 7) - PARTS, here & (LANES - 1)
        values = [jnp.zeros((8, LANES), F32) for _ in groups]
        for p in range(PARTS):
            match = block == p
            for i, r in enumerate(groups):
                found = jnp.take_along_axis(border_ref[p, r : r + 8, :], lane, axis=1)
                values[i] = jnp.where(match, found, values[i])
        columns.append(jnp.concatenate(values, axis=0))
    return jnp.concatenate(columns, axis=1)


def scatter(flows, highs, hots):
    sides = []
    for t in range(2):
        signed = flows if t == 0 else -flows
        sides += [
            jnp.concatenate(
                [signed * jnp.where(highs[t] == a, 1.0, 0.0).astype(BF) for a in range(HIGHS)], axis=0
            )
        ]
    return lax.dot_general(
        jnp.concatenate(sides, axis=1),
        jnp.concatenate(hots, axis=1),
        (((1,), (1,)), ((), ())),
        preferred_element_type=F32,
    )


def put_blocks(acc_ref, out_ref):
    for a in range(HIGHS):
        base = a * 4 * ROWS
        total = acc_ref[base : base + 2 * ROWS, :] + acc_ref[base + 2 * ROWS : base + 4 * ROWS, :]
        for k in range(PER):
            out_ref[a * PER + k] = total[:, k * LANES : (k + 1) * LANES]


def tiles():
    return [slice(first, first + TILE) for first in range(0, NE, TILE)]


def own_across_kernel(volt_ref, term_ref, across_ref, table_ref):
    fill_table([volt_ref[:, a * LOW : (a + 1) * LOW] for a in range(HIGHS)], table_ref)
    for cols in tiles():
        ends = []
        for t in range(2):
            node = term_ref[t : t + 1, cols]
            ends.append(gather(table_ref, node >> SHIFT, one_hot(node & (LOW - 1))))
        across_ref[:, cols] = ends[0] - ends[1]


def flows_of(across, cur_ref, chg_ref, cols):
    current = cur_ref[0:1, cols] * across + cur_ref[1:2, cols] * jnp.tanh(2.0 * across)
    charge = chg_ref[0:1, cols] * across + chg_ref[1:2, cols] * jnp.tanh(across)
    return jnp.concatenate(split(jnp.concatenate([current, charge], axis=0)), axis=0)


def add_up(front, acc_ref):
    count = NE // TILE
    now = front(0)
    for i in range(count):
        later = front(i + 1) if i + 1 < count else None
        part = scatter(*now)
        acc_ref[...] = part if i == 0 else acc_ref[...] + part
        now = later


def flow_kernel(border_ref, own_ref, term_ref, cur_ref, chg_ref, out_ref, across_ref, table_ref, acc_ref):
    blocks = [
        jnp.concatenate([border_ref[a * PER + k] for k in range(PER)], axis=1) for a in range(HIGHS)
    ]
    fill_table(blocks, table_ref)

    def front(i):
        cols = tiles()[i]
        highs, hots, ends = [], [], []
        for t in range(2):
            node = term_ref[t : t + 1, cols]
            highs.append((node >> SHIFT) - HIGHS)
            hots.append(one_hot(node & (LOW - 1)))
            ends.append(lane_gather(border_ref, node) if i else gather(table_ref, highs[t], hots[t]))
        across = own_ref[:, cols] + (ends[0] - ends[1])
        across_ref[:, cols] = across
        return flows_of(across, cur_ref, chg_ref, cols), highs, hots

    add_up(front, acc_ref)
    put_blocks(acc_ref, out_ref)


def own_flow_kernel(across_ref, term_ref, cur_ref, chg_ref, own_ref, acc_ref):
    def front(i):
        cols = tiles()[i]
        highs, hots = [], []
        for t in range(2):
            node = term_ref[t : t + 1, cols]
            highs.append(node >> SHIFT)
            hots.append(one_hot(node & (LOW - 1)))
        return flows_of(across_ref[:, cols], cur_ref, chg_ref, cols), highs, hots

    add_up(front, acc_ref)
    put_blocks(acc_ref, own_ref)


def transform_kernel(flow_ref, high_ref, low_ref, out_ref):
    hi, lo = split(flow_ref[...])
    dot = functools.partial(jnp.dot, preferred_element_type=F32)
    out_ref[...] = dot(high_ref[...], hi) + (dot(high_ref[...], lo) + dot(low_ref[...], hi))


def step_kernel(coef_ref, src_ref, jac_ref, res_ref, raw_ref, sums_ref):
    even = lax.broadcasted_iota(jnp.int32, (ROWS, LANES), 0) % 2 == 0
    raw_sum = jnp.zeros((ROWS, LANES), F32)
    res_sum = jnp.zeros((ROWS, LANES), F32)
    for k in range(NPD // LANES):
        cols = slice(k * LANES, (k + 1) * LANES)
        res = coef_ref[k] - src_ref[:, cols]
        res_ref[:, cols] = res
        first = jnp.where(even, res, pltpu.roll(res, 1, 0))
        second = jnp.where(even, pltpu.roll(res, ROWS - 1, 0), res)
        raw = -(jac_ref[:, 0, cols] * first + jac_ref[:, 1, cols] * second)
        raw_ref[:, cols] = raw
        raw_sum += raw * raw
        res_sum += res * res
    raw_row = jnp.sum(raw_sum, axis=0, keepdims=True)
    res_row = jnp.sum(res_sum, axis=0, keepdims=True)
    half = lax.broadcasted_iota(jnp.int32, (1, LANES), 1) < LANES // 2
    row = jnp.where(half, raw_row + pltpu.roll(raw_row, LANES // 2, 1), res_row + pltpu.roll(res_row, LANES // 2, 1))
    sums_ref[...] = jnp.broadcast_to(row, sums_ref.shape)


def scale_kernel(raw_ref, sums_ref, out_ref, norm_ref):
    row = jnp.sum(sums_ref[...], axis=0, keepdims=True)
    half = lax.broadcasted_iota(jnp.int32, (1, LANES), 1) < LANES // 2
    raw_sum = jnp.sum(jnp.where(half, row, 0.0), axis=1, keepdims=True)
    res_sum = jnp.sum(jnp.where(half, 0.0, row), axis=1, keepdims=True)
    spread = jnp.sqrt(raw_sum / (S * NPD * PARTS) + 1e-06)
    out_ref[...] = raw_ref[...] * jnp.minimum(1.0, trust_radius / spread)
    norm_ref[...] = jnp.sqrt(res_sum)


def call(kernel, out_shapes, scratch=(), limit=24, flops=0):
    return pl.pallas_call(
        kernel,
        out_shape=[jax.ShapeDtypeStruct(s, F32) for s in out_shapes],
        scratch_shapes=list(scratch),
        compiler_params=pltpu.CompilerParams(vmem_limit_bytes=limit * 2**20),
        cost_estimate=pl.CostEstimate(flops=flops, bytes_accessed=2**20, transcendentals=0) if flops else None,
    )


def body(voltages, sources, terminals, elem_current, elem_charge, jacobi):
    sent = jnp.broadcast_to(voltages[None, :, :NB], (PARTS, ROWS, NB))
    border = lax.all_to_all(sent, "dom", 0, 0, tiled=True)
    table_scratch = pltpu.VMEM((2 * HIGHS * ROWS, LOW), BF)
    acc_scratch = pltpu.VMEM((HIGHS * 4 * ROWS, LOW), F32)
    params = (terminals, elem_current, elem_charge)
    (across,) = call(own_across_kernel, [(ROWS, NE)], [table_scratch], 32, 4 * 10**9)(voltages, terminals)
    outgoing, across = call(
        flow_kernel, [(PARTS, 2 * ROWS, LANES), (ROWS, NE)], [table_scratch, acc_scratch], 32, 8 * 10**9
    )(border, across, *params)
    own_call = call(own_flow_kernel, [(PARTS, 2 * ROWS, LANES)], [acc_scratch], 32, 6 * 10**9)
    (own,) = own_call(across, *params)
    incoming = lax.all_to_all(outgoing, "dom", 0, 0, tiled=True)
    own = own.at[0].add(jnp.sum(incoming, axis=0))
    flows = lax.all_to_all(own, "freq", 0, 0, tiled=True).reshape(2 * S, LANES)
    table = transform_table()
    high = table.astype(ml_dtypes.bfloat16)
    low = (table - high.astype(np.float64)).astype(ml_dtypes.bfloat16)
    (coef,) = call(transform_kernel, [(S, LANES)], )(flows, jnp.asarray(high), jnp.asarray(low))
    coef = lax.all_to_all(coef.reshape(PARTS, ROWS, LANES), "freq", 0, 0, tiled=True)
    residual, raw, sums = call(step_kernel, [(ROWS, NPD), (ROWS, NPD), (256, LANES)], )(
        coef, sources, jacobi.reshape(ROWS, 2, NPD)
    )
    sums = lax.all_to_all(sums, ("dom", "freq"), 0, 0, tiled=True)
    newton_step, norm = call(scale_kernel, [(ROWS, NPD), (1, 1)], )(raw, sums)
    return residual, newton_step, norm.reshape(())


def solution(mesh):
    placed = (
        P("freq", "dom"),
        P("freq", "dom"),
        P(None, "dom"),
        P(None, "dom"),
        P(None, "dom"),
        P("freq", None, None, "dom"),
    )
    return jax.shard_map(
        body,
        mesh=mesh,
        in_specs=placed,
        out_specs=(P("freq", "dom"), P("freq", "dom"), P()),
        check_vma=False,
    )
```

```python
import math

import jax
import jax.numpy as jnp
import ml_dtypes
import numpy as np
from jax import lax
from jax.experimental import pallas as pl
from jax.experimental.pallas import tpu as pltpu
from jax.sharding import PartitionSpec as P

S = 512
ROWS = 32
NPD = 2048
NE = 4096
NB = 128
PARTS = 16
LANES = 128
LOW = 512
SHIFT = 9
HIGHS = NPD // LOW
PER = LOW // LANES
TILE = 1024

trust_radius = 2.0
BF = jnp.bfloat16
F32 = jnp.float32


def transform_table():
    row = np.arange(S)
    harmonic = row // 2
    sine = (row % 2 == 1) & (harmonic > 0)
    order = np.where(harmonic == 0, np.where(row % 2 == 1, S // 2, 0), harmonic)
    phase = (order[:, None] * np.arange(S)[None, :] % S) * (2.0 * math.pi / S)
    values = np.where(sine[:, None], np.sin(phase), np.cos(phase))
    weight = np.where(harmonic == 0, math.sqrt(1.0 / S), math.sqrt(2.0 / S))
    forward = values * weight[:, None]
    pairs = forward.reshape(S // 2, 2, S)
    rate = 2.0 / S * np.arange(S // 2)
    derived = (np.stack([pairs[:, 1], -pairs[:, 0]], axis=1) * rate[:, None, None]).reshape(S, S)
    both = np.stack([forward.reshape(S, PARTS, ROWS), derived.reshape(S, PARTS, ROWS)], axis=2)
    return both.reshape(S, 2 * S)


def split(x):
    hi = x.astype(BF)
    return hi, (x - hi.astype(F32)).astype(BF)


def one_hot(low):
    rows = lax.broadcasted_iota(jnp.int32, (256, low.shape[1]), 0).astype(F32).astype(BF)
    parts = []
    for first in range(0, LOW, 256):
        offset = jnp.broadcast_to((low - first).astype(F32).astype(BF), rows.shape)
        parts.append(jnp.where(rows == offset, jnp.ones((), BF), jnp.zeros((), BF)))
    return jnp.concatenate(parts, axis=0)


def fill_table(blocks, table_ref):
    for a, block in enumerate(blocks):
        hi, lo = split(block)
        table_ref[a * ROWS : (a + 1) * ROWS, :] = hi
        table_ref[(HIGHS + a) * ROWS : (HIGHS + a + 1) * ROWS, :] = lo


def gather(table_ref, high, hot):
    found = jnp.dot(table_ref[...], hot, preferred_element_type=F32)
    value = jnp.zeros((ROWS, hot.shape[1]), F32)
    for a in range(HIGHS):
        part = found[a * ROWS : (a + 1) * ROWS] + found[(HIGHS + a) * ROWS : (HIGHS + a + 1) * ROWS]
        value = jnp.where(high == a, part, value)
    return value


def lane_gather(border_ref, node):
    groups = range(0, ROWS, 8)
    columns = []
    for first in range(0, node.shape[1], LANES):
        here = jnp.broadcast_to(node[:, first : first + LANES], (8, LANES))
        block, lane = (here >> 7) - PARTS, here & (LANES - 1)
        values = [jnp.zeros((8, LANES), F32) for _ in groups]
        for p in range(PARTS):
            match = block == p
            for i, r in enumerate(groups):
                found = jnp.take_along_axis(border_ref[p, r : r + 8, :], lane, axis=1)
                values[i] = jnp.where(match, found, values[i])
        columns.append(jnp.concatenate(values, axis=0))
    return jnp.concatenate(columns, axis=1)


def scatter(flows, highs, hots):
    sides = []
    for t in range(2):
        signed = flows if t == 0 else -flows
        sides += [
            jnp.concatenate(
                [signed * jnp.where(highs[t] == a, 1.0, 0.0).astype(BF) for a in range(HIGHS)], axis=0
            )
        ]
    return lax.dot_general(
        jnp.concatenate(sides, axis=1),
        jnp.concatenate(hots, axis=1),
        (((1,), (1,)), ((), ())),
        preferred_element_type=F32,
    )


def put_blocks(acc_ref, out_ref):
    for a in range(HIGHS):
        base = a * 4 * ROWS
        total = acc_ref[base : base + 2 * ROWS, :] + acc_ref[base + 2 * ROWS : base + 4 * ROWS, :]
        for k in range(PER):
            out_ref[a * PER + k] = total[:, k * LANES : (k + 1) * LANES]


def tiles():
    return [slice(first, first + TILE) for first in range(0, NE, TILE)]


def own_across_kernel(volt_ref, term_ref, across_ref, table_ref):
    fill_table([volt_ref[:, a * LOW : (a + 1) * LOW] for a in range(HIGHS)], table_ref)
    for cols in tiles():
        ends = []
        for t in range(2):
            node = term_ref[t : t + 1, cols]
            ends.append(gather(table_ref, node >> SHIFT, one_hot(node & (LOW - 1))))
        across_ref[:, cols] = ends[0] - ends[1]


def flows_of(across, cur_ref, chg_ref, cols):
    current = cur_ref[0:1, cols] * across + cur_ref[1:2, cols] * jnp.tanh(2.0 * across)
    charge = chg_ref[0:1, cols] * across + chg_ref[1:2, cols] * jnp.tanh(across)
    return jnp.concatenate(split(jnp.concatenate([current, charge], axis=0)), axis=0)


def add_up(front, acc_ref):
    count = NE // TILE
    now = front(0)
    for i in range(count):
        later = front(i + 1) if i + 1 < count else None
        part = scatter(*now)
        acc_ref[...] = part if i == 0 else acc_ref[...] + part
        now = later


def flow_kernel(border_ref, own_ref, term_ref, cur_ref, chg_ref, out_ref, across_ref, table_ref, acc_ref):
    blocks = [
        jnp.concatenate([border_ref[a * PER + k] for k in range(PER)], axis=1) for a in range(HIGHS)
    ]
    fill_table(blocks, table_ref)

    def front(i):
        cols = tiles()[i]
        highs, hots, ends = [], [], []
        for t in range(2):
            node = term_ref[t : t + 1, cols]
            highs.append((node >> SHIFT) - HIGHS)
            hots.append(one_hot(node & (LOW - 1)))
            ends.append(lane_gather(border_ref, node) if i else gather(table_ref, highs[t], hots[t]))
        across = own_ref[:, cols] + (ends[0] - ends[1])
        across_ref[:, cols] = across
        return flows_of(across, cur_ref, chg_ref, cols), highs, hots

    add_up(front, acc_ref)
    put_blocks(acc_ref, out_ref)


def own_flow_kernel(across_ref, term_ref, cur_ref, chg_ref, own_ref, acc_ref):
    def front(i):
        cols = tiles()[i]
        highs, hots = [], []
        for t in range(2):
            node = term_ref[t : t + 1, cols]
            highs.append(node >> SHIFT)
            hots.append(one_hot(node & (LOW - 1)))
        return flows_of(across_ref[:, cols], cur_ref, chg_ref, cols), highs, hots

    add_up(front, acc_ref)
    put_blocks(acc_ref, own_ref)


def border_kernel(own_ref, incoming_ref, out_ref):
    total = own_ref[0]
    for p in range(PARTS):
        total = total + incoming_ref[p]
    out_ref[0] = total
    for k in range(1, PARTS):
        out_ref[k] = own_ref[k]


def transform_kernel(flow_ref, high_ref, low_ref, out_ref):
    hi, lo = split(flow_ref[...])
    both = jnp.dot(high_ref[...], jnp.concatenate([hi, lo], axis=1), preferred_element_type=F32)
    rest = jnp.dot(low_ref[...], hi, preferred_element_type=F32)
    out_ref[...] = both[:, :LANES] + (both[:, LANES:] + rest)


def step_kernel(coef_ref, src_ref, jac_ref, res_ref, raw_ref, sums_ref):
    even = lax.broadcasted_iota(jnp.int32, (ROWS, LANES), 0) % 2 == 0
    raw_sum = jnp.zeros((ROWS, LANES), F32)
    res_sum = jnp.zeros((ROWS, LANES), F32)
    for k in range(NPD // LANES):
        cols = slice(k * LANES, (k + 1) * LANES)
        res = coef_ref[k] - src_ref[:, cols]
        res_ref[:, cols] = res
        first = jnp.where(even, res, pltpu.roll(res, 1, 0))
        second = jnp.where(even, pltpu.roll(res, ROWS - 1, 0), res)
        raw = -(jac_ref[:, 0, cols] * first + jac_ref[:, 1, cols] * second)
        raw_ref[:, cols] = raw
        raw_sum += raw * raw
        res_sum += res * res
    raw_row = jnp.sum(raw_sum, axis=0, keepdims=True)
    res_row = jnp.sum(res_sum, axis=0, keepdims=True)
    half = lax.broadcasted_iota(jnp.int32, (1, LANES), 1) < LANES // 2
    row = jnp.where(half, raw_row + pltpu.roll(raw_row, LANES // 2, 1), res_row + pltpu.roll(res_row, LANES // 2, 1))
    sums_ref[...] = jnp.broadcast_to(row, sums_ref.shape)


def scale_kernel(raw_ref, sums_ref, out_ref, norm_ref):
    row = jnp.sum(sums_ref[...], axis=0, keepdims=True)
    half = lax.broadcasted_iota(jnp.int32, (1, LANES), 1) < LANES // 2
    raw_sum = jnp.sum(jnp.where(half, row, 0.0), axis=1, keepdims=True)
    res_sum = jnp.sum(jnp.where(half, 0.0, row), axis=1, keepdims=True)
    spread = jnp.sqrt(raw_sum / (S * NPD * PARTS) + 1e-06)
    out_ref[...] = raw_ref[...] * jnp.minimum(1.0, trust_radius / spread)
    norm_ref[...] = jnp.sqrt(res_sum)


def call(kernel, out_shapes, scratch=(), limit=24, flops=0):
    return pl.pallas_call(
        kernel,
        out_shape=[jax.ShapeDtypeStruct(s, F32) for s in out_shapes],
        scratch_shapes=list(scratch),
        compiler_params=pltpu.CompilerParams(vmem_limit_bytes=limit * 2**20),
        cost_estimate=pl.CostEstimate(flops=flops, bytes_accessed=2**20, transcendentals=0) if flops else None,
    )


def body(voltages, sources, terminals, elem_current, elem_charge, jacobi):
    sent = jnp.broadcast_to(voltages[None, :, :NB], (PARTS, ROWS, NB))
    border = lax.all_to_all(sent, "dom", 0, 0, tiled=True)
    table_scratch = pltpu.VMEM((2 * HIGHS * ROWS, LOW), BF)
    acc_scratch = pltpu.VMEM((HIGHS * 4 * ROWS, LOW), F32)
    params = (terminals, elem_current, elem_charge)
    (across,) = call(own_across_kernel, [(ROWS, NE)], [table_scratch], 32, 4 * 10**9)(voltages, terminals)
    outgoing, across = call(
        flow_kernel, [(PARTS, 2 * ROWS, LANES), (ROWS, NE)], [table_scratch, acc_scratch], 32, 8 * 10**9
    )(border, across, *params)
    own_call = call(own_flow_kernel, [(PARTS, 2 * ROWS, LANES)], [acc_scratch], 32, 6 * 10**9)
    (own,) = own_call(across, *params)
    incoming = lax.all_to_all(outgoing, "dom", 0, 0, tiled=True)
    own = pl.pallas_call(
        border_kernel,
        out_shape=jax.ShapeDtypeStruct(own.shape, F32),

        in_specs=[pl.BlockSpec(memory_space=pltpu.VMEM)] * 2,
        out_specs=pl.BlockSpec(memory_space=pltpu.VMEM),
        compiler_params=pltpu.CompilerParams(vmem_limit_bytes=8 * 2**20),
    )(own, incoming)
    flows = lax.all_to_all(own, "freq", 0, 0, tiled=True).reshape(2 * S, LANES)
    table = transform_table()
    high = table.astype(ml_dtypes.bfloat16)
    low = (table - high.astype(np.float64)).astype(ml_dtypes.bfloat16)
    (coef,) = call(transform_kernel, [(S, LANES)], )(flows, jnp.asarray(high), jnp.asarray(low))
    coef = lax.all_to_all(coef.reshape(PARTS, ROWS, LANES), "freq", 0, 0, tiled=True)
    residual, raw, sums = call(step_kernel, [(ROWS, NPD), (ROWS, NPD), (256, LANES)], )(
        coef, sources, jacobi.reshape(ROWS, 2, NPD)
    )
    sums = lax.all_to_all(sums, ("dom", "freq"), 0, 0, tiled=True)
    newton_step, norm = call(scale_kernel, [(ROWS, NPD), (1, 1)], )(raw, sums)
    return residual, newton_step, norm.reshape(())


def solution(mesh):
    placed = (
        P("freq", "dom"),
        P("freq", "dom"),
        P(None, "dom"),
        P(None, "dom"),
        P(None, "dom"),
        P("freq", None, None, "dom"),
    )
    return jax.shard_map(
        body,
        mesh=mesh,
        in_specs=placed,
        out_specs=(P("freq", "dom"), P("freq", "dom"), P()),
        check_vma=False,
    )
```

```python
import math

import jax
import jax.numpy as jnp
import ml_dtypes
import numpy as np
from jax import lax
from jax.experimental import pallas as pl
from jax.experimental.pallas import tpu as pltpu
from jax.sharding import PartitionSpec as P

S = 512
ROWS = 32
NPD = 2048
NE = 4096
NB = 128
PARTS = 16
LANES = 128
LOW = 512
SHIFT = 9
HIGHS = NPD // LOW
PER = LOW // LANES
TILE = 1024

trust_radius = 2.0
BF = jnp.bfloat16
F32 = jnp.float32


def transform_table():
    row = np.arange(S)
    harmonic = row // 2
    sine = (row % 2 == 1) & (harmonic > 0)
    order = np.where(harmonic == 0, np.where(row % 2 == 1, S // 2, 0), harmonic)
    phase = (order[:, None] * np.arange(S)[None, :] % S) * (2.0 * math.pi / S)
    values = np.where(sine[:, None], np.sin(phase), np.cos(phase))
    weight = np.where(harmonic == 0, math.sqrt(1.0 / S), math.sqrt(2.0 / S))
    forward = values * weight[:, None]
    pairs = forward.reshape(S // 2, 2, S)
    rate = 2.0 / S * np.arange(S // 2)
    derived = (np.stack([pairs[:, 1], -pairs[:, 0]], axis=1) * rate[:, None, None]).reshape(S, S)
    both = np.stack([forward.reshape(S, PARTS, ROWS), derived.reshape(S, PARTS, ROWS)], axis=2)
    return both.reshape(S, 2 * S)


def split(x):
    hi = x.astype(BF)
    return hi, (x - hi.astype(F32)).astype(BF)


def one_hot(low):
    rows = lax.broadcasted_iota(jnp.int32, (256, low.shape[1]), 0).astype(F32).astype(BF)
    parts = []
    for first in range(0, LOW, 256):
        offset = jnp.broadcast_to((low - first).astype(F32).astype(BF), rows.shape)
        parts.append(jnp.where(rows == offset, jnp.ones((), BF), jnp.zeros((), BF)))
    return jnp.concatenate(parts, axis=0)


def fill_table(blocks, table_ref):
    for a, block in enumerate(blocks):
        hi, lo = split(block)
        table_ref[a * ROWS : (a + 1) * ROWS, :] = hi
        table_ref[(HIGHS + a) * ROWS : (HIGHS + a + 1) * ROWS, :] = lo


def gather(table_ref, high, hot):
    found = jnp.dot(table_ref[...], hot, preferred_element_type=F32)
    value = jnp.zeros((ROWS, hot.shape[1]), F32)
    for a in range(HIGHS):
        part = found[a * ROWS : (a + 1) * ROWS] + found[(HIGHS + a) * ROWS : (HIGHS + a + 1) * ROWS]
        value = jnp.where(high == a, part, value)
    return value


def lane_gather(border_ref, node):
    groups = range(0, ROWS, 8)
    columns = []
    for first in range(0, node.shape[1], LANES):
        here = jnp.broadcast_to(node[:, first : first + LANES], (8, LANES))
        block, lane = (here >> 7) - PARTS, here & (LANES - 1)
        values = [jnp.zeros((8, LANES), F32) for _ in groups]
        for p in range(PARTS):
            match = block == p
            for i, r in enumerate(groups):
                found = jnp.take_along_axis(border_ref[p, r : r + 8, :], lane, axis=1)
                values[i] = jnp.where(match, found, values[i])
        columns.append(jnp.concatenate(values, axis=0))
    return jnp.concatenate(columns, axis=1)


def scatter(flows, highs, hots):
    sides = []
    for t in range(2):
        signed = flows if t == 0 else -flows
        sides += [
            jnp.concatenate(
                [signed * jnp.where(highs[t] == a, 1.0, 0.0).astype(BF) for a in range(HIGHS)], axis=0
            )
        ]
    return lax.dot_general(
        jnp.concatenate(sides, axis=1),
        jnp.concatenate(hots, axis=1),
        (((1,), (1,)), ((), ())),
        preferred_element_type=F32,
    )


def put_blocks(acc_ref, out_ref):
    for a in range(HIGHS):
        base = a * 4 * ROWS
        total = acc_ref[base : base + 2 * ROWS, :] + acc_ref[base + 2 * ROWS : base + 4 * ROWS, :]
        for k in range(PER):
            out_ref[a * PER + k] = total[:, k * LANES : (k + 1) * LANES]


def tiles():
    return [slice(first, first + TILE) for first in range(0, NE, TILE)]


def own_across_kernel(volt_ref, term_ref, across_ref, table_ref):
    fill_table([volt_ref[:, a * LOW : (a + 1) * LOW] for a in range(HIGHS)], table_ref)
    for cols in tiles():
        ends = []
        for t in range(2):
            node = term_ref[t : t + 1, cols]
            ends.append(gather(table_ref, node >> SHIFT, one_hot(node & (LOW - 1))))
        across_ref[:, cols] = ends[0] - ends[1]


def flows_of(across, cur_ref, chg_ref, cols):
    current = cur_ref[0:1, cols] * across + cur_ref[1:2, cols] * jnp.tanh(2.0 * across)
    charge = chg_ref[0:1, cols] * across + chg_ref[1:2, cols] * jnp.tanh(across)
    return jnp.concatenate(split(jnp.concatenate([current, charge], axis=0)), axis=0)


def add_up(front, acc_ref):
    count = NE // TILE
    now = front(0)
    for i in range(count):
        later = front(i + 1) if i + 1 < count else None
        part = scatter(*now)
        acc_ref[...] = part if i == 0 else acc_ref[...] + part
        now = later


def flow_kernel(border_ref, own_ref, term_ref, cur_ref, chg_ref, out_ref, across_ref, table_ref, acc_ref):
    blocks = [
        jnp.concatenate([border_ref[a * PER + k] for k in range(PER)], axis=1) for a in range(HIGHS)
    ]
    fill_table(blocks, table_ref)

    def front(i):
        cols = tiles()[i]
        highs, hots, ends = [], [], []
        for t in range(2):
            node = term_ref[t : t + 1, cols]
            highs.append((node >> SHIFT) - HIGHS)
            hots.append(one_hot(node & (LOW - 1)))
            ends.append(lane_gather(border_ref, node) if i else gather(table_ref, highs[t], hots[t]))
        across = own_ref[:, cols] + (ends[0] - ends[1])
        across_ref[:, cols] = across
        return flows_of(across, cur_ref, chg_ref, cols), highs, hots

    add_up(front, acc_ref)
    put_blocks(acc_ref, out_ref)


def own_flow_kernel(across_ref, term_ref, cur_ref, chg_ref, own_ref, acc_ref):
    def front(i):
        cols = tiles()[i]
        highs, hots = [], []
        for t in range(2):
            node = term_ref[t : t + 1, cols]
            highs.append(node >> SHIFT)
            hots.append(one_hot(node & (LOW - 1)))
        return flows_of(across_ref[:, cols], cur_ref, chg_ref, cols), highs, hots

    add_up(front, acc_ref)
    put_blocks(acc_ref, own_ref)


def border_kernel(own_ref, incoming_ref, out_ref):
    total = own_ref[0]
    for p in range(PARTS):
        total = total + incoming_ref[p]
    out_ref[0] = total
    for k in range(1, PARTS):
        out_ref[k] = own_ref[k]


def transform_kernel(flow_ref, high_ref, low_ref, out_ref):
    hi, lo = split(flow_ref[...])
    both = jnp.dot(high_ref[...], jnp.concatenate([hi, lo], axis=1), preferred_element_type=F32)
    rest = jnp.dot(low_ref[...], hi, preferred_element_type=F32)
    out_ref[...] = both[:, :LANES] + (both[:, LANES:] + rest)


def step_kernel(coef_ref, src_ref, jac_ref, res_ref, raw_ref, sums_ref):
    even = lax.broadcasted_iota(jnp.int32, (ROWS, LANES), 0) % 2 == 0
    raw_sum = jnp.zeros((ROWS, LANES), F32)
    res_sum = jnp.zeros((ROWS, LANES), F32)
    for k in range(NPD // LANES):
        cols = slice(k * LANES, (k + 1) * LANES)
        res = coef_ref[k] - src_ref[:, cols]
        res_ref[:, cols] = res
        first = jnp.where(even, res, pltpu.roll(res, 1, 0))
        second = jnp.where(even, pltpu.roll(res, ROWS - 1, 0), res)
        raw = -(jac_ref[:, 0, cols] * first + jac_ref[:, 1, cols] * second)
        raw_ref[:, cols] = raw
        raw_sum += raw * raw
        res_sum += res * res
    raw_row = jnp.sum(raw_sum, axis=0, keepdims=True)
    res_row = jnp.sum(res_sum, axis=0, keepdims=True)
    half = lax.broadcasted_iota(jnp.int32, (1, LANES), 1) < LANES // 2
    row = jnp.where(half, raw_row + pltpu.roll(raw_row, LANES // 2, 1), res_row + pltpu.roll(res_row, LANES // 2, 1))
    sums_ref[...] = jnp.broadcast_to(row, sums_ref.shape)


def scale_kernel(res_ref, raw_ref, sums_ref, res_out_ref, out_ref, norm_ref):
    res_out_ref[...] = res_ref[...]
    row = jnp.sum(sums_ref[...], axis=0, keepdims=True)
    half = lax.broadcasted_iota(jnp.int32, (1, LANES), 1) < LANES // 2
    raw_sum = jnp.sum(jnp.where(half, row, 0.0), axis=1, keepdims=True)
    res_sum = jnp.sum(jnp.where(half, 0.0, row), axis=1, keepdims=True)
    spread = jnp.sqrt(raw_sum / (S * NPD * PARTS) + 1e-06)
    out_ref[...] = raw_ref[...] * jnp.minimum(1.0, trust_radius / spread)
    norm_ref[...] = jnp.sqrt(res_sum)


def call(kernel, out_shapes, scratch=(), limit=24, flops=0):
    return pl.pallas_call(
        kernel,
        out_shape=[jax.ShapeDtypeStruct(s, F32) for s in out_shapes],
        scratch_shapes=list(scratch),
        compiler_params=pltpu.CompilerParams(vmem_limit_bytes=limit * 2**20),
        cost_estimate=pl.CostEstimate(flops=flops, bytes_accessed=2**20, transcendentals=0) if flops else None,
    )


def body(voltages, sources, terminals, elem_current, elem_charge, jacobi):
    sent = jnp.broadcast_to(voltages[None, :, :NB], (PARTS, ROWS, NB))
    border = lax.all_to_all(sent, "dom", 0, 0, tiled=True)
    table_scratch = pltpu.VMEM((2 * HIGHS * ROWS, LOW), BF)
    acc_scratch = pltpu.VMEM((HIGHS * 4 * ROWS, LOW), F32)
    params = (terminals, elem_current, elem_charge)
    (across,) = call(own_across_kernel, [(ROWS, NE)], [table_scratch], 32, 4 * 10**9)(voltages, terminals)
    outgoing, across = call(
        flow_kernel, [(PARTS, 2 * ROWS, LANES), (ROWS, NE)], [table_scratch, acc_scratch], 32, 8 * 10**9
    )(border, across, *params)
    own_call = call(own_flow_kernel, [(PARTS, 2 * ROWS, LANES)], [acc_scratch], 32, 6 * 10**9)
    (own,) = own_call(across, *params)
    incoming = lax.all_to_all(outgoing, "dom", 0, 0, tiled=True)
    own = pl.pallas_call(
        border_kernel,
        out_shape=jax.ShapeDtypeStruct(own.shape, F32),
        in_specs=[pl.BlockSpec(memory_space=pltpu.VMEM)] * 2,
        out_specs=pl.BlockSpec(memory_space=pltpu.VMEM),
        compiler_params=pltpu.CompilerParams(vmem_limit_bytes=8 * 2**20),
    )(own, incoming)
    flows = lax.all_to_all(own, "freq", 0, 0, tiled=True).reshape(2 * S, LANES)
    table = transform_table()
    high = table.astype(ml_dtypes.bfloat16)
    low = (table - high.astype(np.float64)).astype(ml_dtypes.bfloat16)
    (coef,) = call(transform_kernel, [(S, LANES)], (), 12)(flows, jnp.asarray(high), jnp.asarray(low))
    coef = lax.all_to_all(coef.reshape(PARTS, ROWS, LANES), "freq", 0, 0, tiled=True)
    residual, raw, sums = call(step_kernel, [(ROWS, NPD), (ROWS, NPD), (256, LANES)], (), 12)(
        coef, sources, jacobi.reshape(ROWS, 2, NPD)
    )
    sums = lax.all_to_all(sums, ("dom", "freq"), 0, 0, tiled=True)
    residual, newton_step, norm = call(scale_kernel, [(ROWS, NPD), (ROWS, NPD), (1, 1)], (), 12)(
        residual, raw, sums
    )
    return residual, newton_step, norm.reshape(())


def solution(mesh):
    placed = (
        P("freq", "dom"),
        P("freq", "dom"),
        P(None, "dom"),
        P(None, "dom"),
        P(None, "dom"),
        P("freq", None, None, "dom"),
    )
    return jax.shard_map(
        body,
        mesh=mesh,
        in_specs=placed,
        out_specs=(P("freq", "dom"), P("freq", "dom"), P()),
        check_vma=False,
    )
```

```python
import math

import jax
import jax.numpy as jnp
import ml_dtypes
import numpy as np
from jax import lax
from jax.experimental import pallas as pl
from jax.experimental.pallas import tpu as pltpu
from jax.sharding import PartitionSpec as P

S = 512
ROWS = 32
NPD = 2048
NE = 4096
NB = 128
PARTS = 16
LANES = 128
LOW = 512
SHIFT = 9
HIGHS = NPD // LOW
PER = LOW // LANES
TILE = 1024
FLOW_TILES = (768, 896, 896, 896, 640)

trust_radius = 2.0
BF = jnp.bfloat16
F32 = jnp.float32


def transform_table():
    row = np.arange(S)
    harmonic = row // 2
    sine = (row % 2 == 1) & (harmonic > 0)
    order = np.where(harmonic == 0, np.where(row % 2 == 1, S // 2, 0), harmonic)
    phase = (order[:, None] * np.arange(S)[None, :] % S) * (2.0 * math.pi / S)
    values = np.where(sine[:, None], np.sin(phase), np.cos(phase))
    weight = np.where(harmonic == 0, math.sqrt(1.0 / S), math.sqrt(2.0 / S))
    forward = values * weight[:, None]
    pairs = forward.reshape(S // 2, 2, S)
    rate = 2.0 / S * np.arange(S // 2)
    derived = (np.stack([pairs[:, 1], -pairs[:, 0]], axis=1) * rate[:, None, None]).reshape(S, S)
    both = np.stack([forward.reshape(S, PARTS, ROWS), derived.reshape(S, PARTS, ROWS)], axis=2)
    return both.reshape(S, 2 * S)


def split(x):
    hi = x.astype(BF)
    return hi, (x - hi.astype(F32)).astype(BF)


def one_hot(low):
    rows = lax.broadcasted_iota(jnp.int32, (256, low.shape[1]), 0).astype(F32).astype(BF)
    parts = []
    for first in range(0, LOW, 256):
        offset = jnp.broadcast_to((low - first).astype(F32).astype(BF), rows.shape)
        parts.append(jnp.where(rows == offset, jnp.ones((), BF), jnp.zeros((), BF)))
    return jnp.concatenate(parts, axis=0)


def fill_table(blocks, table_ref):
    for a, block in enumerate(blocks):
        hi, lo = split(block)
        table_ref[a * ROWS : (a + 1) * ROWS, :] = hi
        table_ref[(HIGHS + a) * ROWS : (HIGHS + a + 1) * ROWS, :] = lo


def gather(table_ref, high, hot):
    found = jnp.dot(table_ref[...], hot, preferred_element_type=F32)
    value = jnp.zeros((ROWS, hot.shape[1]), F32)
    for a in range(HIGHS):
        part = found[a * ROWS : (a + 1) * ROWS] + found[(HIGHS + a) * ROWS : (HIGHS + a + 1) * ROWS]
        value = jnp.where(high == a, part, value)
    return value


def lane_gather(border_ref, node):
    groups = range(0, ROWS, 8)
    columns = []
    for first in range(0, node.shape[1], LANES):
        here = jnp.broadcast_to(node[:, first : first + LANES], (8, LANES))
        block, lane = (here >> 7) - PARTS, here & (LANES - 1)
        values = [jnp.zeros((8, LANES), F32) for _ in groups]
        for p in range(PARTS):
            match = block == p
            for i, r in enumerate(groups):
                found = jnp.take_along_axis(border_ref[p, r : r + 8, :], lane, axis=1)
                values[i] = jnp.where(match, found, values[i])
        columns.append(jnp.concatenate(values, axis=0))
    return jnp.concatenate(columns, axis=1)


def scatter(flows, highs, hots):
    sides = []
    for t in range(2):
        signed = flows if t == 0 else -flows
        sides += [
            jnp.concatenate(
                [signed * jnp.where(highs[t] == a, 1.0, 0.0).astype(BF) for a in range(HIGHS)], axis=0
            )
        ]
    return lax.dot_general(
        jnp.concatenate(sides, axis=1),
        jnp.concatenate(hots, axis=1),
        (((1,), (1,)), ((), ())),
        preferred_element_type=F32,
    )


def put_blocks(acc_ref, out_ref):
    for a in range(HIGHS):
        base = a * 4 * ROWS
        total = acc_ref[base : base + 2 * ROWS, :] + acc_ref[base + 2 * ROWS : base + 4 * ROWS, :]
        for k in range(PER):
            out_ref[a * PER + k] = total[:, k * LANES : (k + 1) * LANES]


def tiles(sizes=(TILE,) * (NE // TILE)):
    ends = [sum(sizes[: i + 1]) for i in range(len(sizes))]
    return [slice(end - size, end) for size, end in zip(sizes, ends, strict=True)]


def own_across_kernel(volt_ref, term_ref, across_ref, table_ref):
    fill_table([volt_ref[:, a * LOW : (a + 1) * LOW] for a in range(HIGHS)], table_ref)
    for cols in tiles():
        ends = []
        for t in range(2):
            node = term_ref[t : t + 1, cols]
            ends.append(gather(table_ref, node >> SHIFT, one_hot(node & (LOW - 1))))
        across_ref[:, cols] = ends[0] - ends[1]


def flows_of(across, cur_ref, chg_ref, cols):
    current = cur_ref[0:1, cols] * across + cur_ref[1:2, cols] * jnp.tanh(2.0 * across)
    charge = chg_ref[0:1, cols] * across + chg_ref[1:2, cols] * jnp.tanh(across)
    return jnp.concatenate(split(jnp.concatenate([current, charge], axis=0)), axis=0)


def add_up(front, count, acc_ref):
    now = front(0)
    for i in range(count):
        later = front(i + 1) if i + 1 < count else None
        part = scatter(*now)
        acc_ref[...] = part if i == 0 else acc_ref[...] + part
        now = later


def flow_kernel(border_ref, own_ref, term_ref, cur_ref, chg_ref, out_ref, across_ref, table_ref, acc_ref):
    blocks = [
        jnp.concatenate([border_ref[a * PER + k] for k in range(PER)], axis=1) for a in range(HIGHS)
    ]
    fill_table(blocks, table_ref)

    def front(i):
        cols = tiles(FLOW_TILES)[i]
        highs, hots, ends = [], [], []
        for t in range(2):
            node = term_ref[t : t + 1, cols]
            highs.append((node >> SHIFT) - HIGHS)
            hots.append(one_hot(node & (LOW - 1)))
            ends.append(lane_gather(border_ref, node) if i else gather(table_ref, highs[t], hots[t]))
        across = own_ref[:, cols] + (ends[0] - ends[1])
        across_ref[:, cols] = across
        return flows_of(across, cur_ref, chg_ref, cols), highs, hots

    add_up(front, len(FLOW_TILES), acc_ref)
    put_blocks(acc_ref, out_ref)


def own_flow_kernel(across_ref, term_ref, cur_ref, chg_ref, own_ref, acc_ref):
    def front(i):
        cols = tiles()[i]
        highs, hots = [], []
        for t in range(2):
            node = term_ref[t : t + 1, cols]
            highs.append(node >> SHIFT)
            hots.append(one_hot(node & (LOW - 1)))
        return flows_of(across_ref[:, cols], cur_ref, chg_ref, cols), highs, hots

    add_up(front, NE // TILE, acc_ref)
    put_blocks(acc_ref, own_ref)


def border_kernel(own_ref, incoming_ref, out_ref):
    total = own_ref[0]
    for p in range(PARTS):
        total = total + incoming_ref[p]
    out_ref[0] = total
    for k in range(1, PARTS):
        out_ref[k] = own_ref[k]


def transform_kernel(flow_ref, high_ref, low_ref, out_ref):
    hi, lo = split(flow_ref[...])
    both = jnp.dot(high_ref[...], jnp.concatenate([hi, lo], axis=1), preferred_element_type=F32)
    rest = jnp.dot(low_ref[...], hi, preferred_element_type=F32)
    out_ref[...] = both[:, :LANES] + (both[:, LANES:] + rest)


def step_kernel(coef_ref, src_ref, jac_ref, res_ref, raw_ref, sums_ref):
    even = lax.broadcasted_iota(jnp.int32, (ROWS, LANES), 0) % 2 == 0
    raw_sum = jnp.zeros((ROWS, LANES), F32)
    res_sum = jnp.zeros((ROWS, LANES), F32)
    for k in range(NPD // LANES):
        cols = slice(k * LANES, (k + 1) * LANES)
        res = coef_ref[k] - src_ref[:, cols]
        res_ref[:, cols] = res
        first = jnp.where(even, res, pltpu.roll(res, 1, 0))
        second = jnp.where(even, pltpu.roll(res, ROWS - 1, 0), res)
        raw = -(jac_ref[:, 0, cols] * first + jac_ref[:, 1, cols] * second)
        raw_ref[:, cols] = raw
        raw_sum += raw * raw
        res_sum += res * res
    raw_row = jnp.sum(raw_sum, axis=0, keepdims=True)
    res_row = jnp.sum(res_sum, axis=0, keepdims=True)
    half = lax.broadcasted_iota(jnp.int32, (1, LANES), 1) < LANES // 2
    row = jnp.where(half, raw_row + pltpu.roll(raw_row, LANES // 2, 1), res_row + pltpu.roll(res_row, LANES // 2, 1))
    sums_ref[...] = jnp.broadcast_to(row, sums_ref.shape)


def scale_kernel(res_ref, raw_ref, sums_ref, res_out_ref, out_ref, norm_ref):
    res_out_ref[...] = res_ref[...]
    row = jnp.sum(sums_ref[...], axis=0, keepdims=True)
    half = lax.broadcasted_iota(jnp.int32, (1, LANES), 1) < LANES // 2
    raw_sum = jnp.sum(jnp.where(half, row, 0.0), axis=1, keepdims=True)
    res_sum = jnp.sum(jnp.where(half, 0.0, row), axis=1, keepdims=True)
    spread = jnp.sqrt(raw_sum / (S * NPD * PARTS) + 1e-06)
    out_ref[...] = raw_ref[...] * jnp.minimum(1.0, trust_radius / spread)
    norm_ref[...] = jnp.sqrt(res_sum)


def call(kernel, out_shapes, scratch=(), limit=24, flops=0):
    return pl.pallas_call(
        kernel,
        out_shape=[jax.ShapeDtypeStruct(s, F32) for s in out_shapes],
        scratch_shapes=list(scratch),
        compiler_params=pltpu.CompilerParams(vmem_limit_bytes=limit * 2**20),
        cost_estimate=pl.CostEstimate(flops=flops, bytes_accessed=2**20, transcendentals=0) if flops else None,
    )


def body(voltages, sources, terminals, elem_current, elem_charge, jacobi):
    sent = jnp.broadcast_to(voltages[None, :, :NB], (PARTS, ROWS, NB))
    border = lax.all_to_all(sent, "dom", 0, 0, tiled=True)
    table_scratch = pltpu.VMEM((2 * HIGHS * ROWS, LOW), BF)
    acc_scratch = pltpu.VMEM((HIGHS * 4 * ROWS, LOW), F32)
    params = (terminals, elem_current, elem_charge)
    (across,) = call(own_across_kernel, [(ROWS, NE)], [table_scratch], 32, 4 * 10**9)(voltages, terminals)
    outgoing, across = call(
        flow_kernel, [(PARTS, 2 * ROWS, LANES), (ROWS, NE)], [table_scratch, acc_scratch], 32, 8 * 10**9
    )(border, across, *params)
    own_call = call(own_flow_kernel, [(PARTS, 2 * ROWS, LANES)], [acc_scratch], 32, 6 * 10**9)
    (own,) = own_call(across, *params)
    incoming = lax.all_to_all(outgoing, "dom", 0, 0, tiled=True)
    own = pl.pallas_call(
        border_kernel,
        out_shape=jax.ShapeDtypeStruct(own.shape, F32),
        in_specs=[pl.BlockSpec(memory_space=pltpu.VMEM)] * 2,
        out_specs=pl.BlockSpec(memory_space=pltpu.VMEM),
        compiler_params=pltpu.CompilerParams(vmem_limit_bytes=8 * 2**20),
    )(own, incoming)
    flows = lax.all_to_all(own, "freq", 0, 0, tiled=True).reshape(2 * S, LANES)
    table = transform_table()
    high = table.astype(ml_dtypes.bfloat16)
    low = (table - high.astype(np.float64)).astype(ml_dtypes.bfloat16)
    (coef,) = call(transform_kernel, [(S, LANES)], (), 12)(flows, jnp.asarray(high), jnp.asarray(low))
    coef = lax.all_to_all(coef.reshape(PARTS, ROWS, LANES), "freq", 0, 0, tiled=True)
    residual, raw, sums = call(step_kernel, [(ROWS, NPD), (ROWS, NPD), (256, LANES)], (), 12)(
        coef, sources, jacobi.reshape(ROWS, 2, NPD)
    )
    sums = lax.all_to_all(sums, ("dom", "freq"), 0, 0, tiled=True)
    residual, newton_step, norm = call(scale_kernel, [(ROWS, NPD), (ROWS, NPD), (1, 1)], (), 12)(
        residual, raw, sums
    )
    return residual, newton_step, norm.reshape(())


def solution(mesh):
    placed = (
        P("freq", "dom"),
        P("freq", "dom"),
        P(None, "dom"),
        P(None, "dom"),
        P(None, "dom"),
        P("freq", None, None, "dom"),
    )
    return jax.shard_map(
        body,
        mesh=mesh,
        in_specs=placed,
        out_specs=(P("freq", "dom"), P("freq", "dom"), P()),
        check_vma=False,
    )
```
